32 devices in a mesh: res: 8 (over z, x), rep: 4 (over y, core).
Axes of the slice: x: 2, y: 2, z: 4, core: 2. Of those that a mesh axis runs over, the one named last changes fastest.
Arguments:
- pair: bfloat16 [4, 384, 384, 128], P('rep', 'res'), may hold values from -64 to 64
- residue_mask: int32 [4, 384], P('rep'), may hold values from 0 to 1, as said below
- bin_targets: int32 [4, 384, 384], P('rep', 'res'), may hold values from 0 to 63
- gain_in: float32 [128], replicated, may hold values from 0.1 to 1.9
- left_proj: bfloat16 [128, 128], replicated, may hold values from -0.5 to 0.5
- left_gate: bfloat16 [128, 128], replicated, may hold values from -0.5 to 0.5
- right_proj: bfloat16 [128, 128], replicated, may hold values from -0.5 to 0.5
- right_gate: bfloat16 [128, 128], replicated, may hold values from -0.5 to 0.5
- gate_weight: bfloat16 [128, 128], replicated, may hold values from -0.5 to 0.5
- gain_out: float32 [128], replicated, may hold values from 0.1 to 1.9
- out_weight: bfloat16 [128, 128], replicated, may hold values from -0.5 to 0.5
- head_weight: bfloat16 [128, 64], replicated, may hold values from -2 to 2
- head_bias: float32 [64], replicated, may hold values from -4 to 4
Outputs:
- updated_pair: bfloat16 [4, 384, 384, 128], P('rep', 'res')
- pair_grad: bfloat16 [4, 384, 384, 128], P('rep', 'res')
- head_grad: float32 [128, 64], replicated
- bias_grad: float32 [64], replicated
- mean_loss: float32 [1], replicated
The draws below stay inside these ranges and needn't reach their ends.
Inputs may be any that keep to these rules, and one draw needn't show every extreme that they name: `residue_mask`: 1 marks a resolved residue; the last residue of each crop is 1.
All inputs are finite; a program needn't handle non-finite values.
Results may differ from the reference program's by a relative error of at most 0.0065.
The reference program's roundings to bfloat16 on the way (of `normed`, `triangle`, `normed_tri`, `symmetric` and `dlogits`) count: a program that leaves them out, or rounds other values in their place, can miss the bound.
Values may be sent and summed in bfloat16 or wider, within the bound.
A program may use at most 128 MiB of HBM per device.

```python
import math
import jax
import jax.numpy as jnp
from jax import lax

LEN = 384
CP = 128
CT = 128
NBINS = 64
CROPS = 4


def draw_pair(key, part):
    key = jax.random.fold_in(key, 11)
    key_list = jax.random.split(key, 3)
    channel_scale = jnp.exp(jax.random.uniform(key_list[0], (CP,), minval=math.log(0.5), maxval=math.log(4.0)))
    row_scale = jnp.exp(jax.random.uniform(key_list[1], (CROPS, LEN, 1, 1), minval=math.log(0.7), maxval=math.log(1.4)))
    base = jnp.clip(jax.random.normal(key_list[2], (CROPS, LEN, LEN, CP)), -4.0, 4.0)
    return (base * channel_scale * row_scale).astype(jnp.bfloat16)


def draw_head_weight(key, part):
    key = jax.random.fold_in(key, 12)
    key_list = jax.random.split(key, 1)
    spread = 2.2 / math.sqrt(CP)
    drawn = jnp.clip(jax.random.normal(key_list[0], (CP, NBINS)), -4.0, 4.0) * spread
    return drawn.astype(jnp.bfloat16)


def draw_residue_mask(key, part):
    key = jax.random.fold_in(key, 13)
    threshold = 300 + 700 * lax.broadcasted_iota(jnp.int32, (1, LEN), 1) // (LEN - 1)
    sample = jax.random.randint(key, (CROPS, LEN), 0, 1000)
    return (sample < threshold).astype(jnp.int32)


def touch_ends(drawn, key, least, high):
    index_at = [jax.random.randint(jax.random.fold_in(key, axis), (), 0, length) for axis, length in enumerate(drawn.shape)]
    main_axis = drawn.shape.index(max(drawn.shape))
    beside = index_at[:main_axis] + [(index_at[main_axis] + 1) % drawn.shape[main_axis]] + index_at[main_axis + 1:]
    return drawn.at[tuple(index_at)].set(least).at[tuple(beside)].set(high)


def centred(stream_key, extent, scale, bound, kind=jnp.bfloat16):
    array = jax.random.normal(stream_key, extent, jnp.float32) * scale
    return jnp.minimum(jnp.maximum(array, -bound), bound).astype(kind)


def setup_inputs(seed: int = 0) -> dict:
    splits = jax.random.split(jax.random.key(seed), 14)
    return {
        "pair": draw_pair(jax.random.fold_in(splits[13], 71), 0),
        "residue_mask": draw_residue_mask(jax.random.fold_in(splits[13], 71), 0),
        "bin_targets": touch_ends(jax.random.randint(splits[2], (CROPS, LEN, LEN), 0, NBINS), jax.random.fold_in(splits[2], 1), 0, NBINS - 1).astype(jnp.int32),
        "gain_in": jnp.clip(1.0 + 0.18 * jax.random.normal(splits[3], (CP,), jnp.float32), 0.1, 1.9),
        "left_proj": centred(splits[4], (CP, CT), CP ** -0.5, 0.5),
        "left_gate": centred(splits[5], (CP, CT), CP ** -0.5, 0.5),
        "right_proj": centred(splits[6], (CP, CT), CP ** -0.5, 0.5),
        "right_gate": centred(splits[7], (CP, CT), CP ** -0.5, 0.5),
        "gate_weight": centred(splits[8], (CP, CP), CP ** -0.5, 0.5),
        "gain_out": jnp.clip(1.0 + 0.18 * jax.random.normal(splits[9], (CT,), jnp.float32), 0.1, 1.9),
        "out_weight": centred(splits[10], (CT, CP), CT ** -0.5, 0.5),
        "head_weight": draw_head_weight(jax.random.fold_in(splits[13], 71), 0),
        "head_bias": centred(splits[12], (NBINS,), 1.0, 4.0, jnp.float32),
    }


def layer_norm(values, reduce_axis):
    average = lax.optimization_barrier(jnp.mean(values, axis=reduce_axis, keepdims=True))
    centered = values - average
    variance = lax.optimization_barrier(jnp.mean(centered * centered, axis=reduce_axis, keepdims=True))
    return centered * lax.rsqrt(variance + 1e-05)

def reference(pair, residue_mask, bin_targets, gain_in, left_proj, left_gate, right_proj, right_gate, gate_weight, gain_out, out_weight, head_weight, head_bias):

    def one_crop(packed):
        crop_pair, crop_mask, crop_targets = packed
        resolved = crop_mask.astype(jnp.float32)
        pair_mask = (resolved[:, None] * resolved[None, :]).reshape(-1)
        pair_float = crop_pair.astype(jnp.float32)
        normed = (layer_norm(pair_float, -1) * gain_in).astype(jnp.bfloat16).reshape(LEN * LEN, CP)

        def factor(project_weight, gating_weight):
            projected = jnp.dot(normed, project_weight, preferred_element_type=jnp.float32)
            gated = jax.nn.sigmoid(jnp.dot(normed, gating_weight, preferred_element_type=jnp.float32))
            return (gated * projected * pair_mask[:, None]).astype(jnp.bfloat16).reshape(LEN, LEN, CT)
        left_factor = factor(left_proj, left_gate)
        right_factor = factor(right_proj, right_gate)
        triangle = jnp.einsum('ikc,jkc->ijc', left_factor.astype(jnp.float32), right_factor.astype(jnp.float32)).astype(jnp.bfloat16)
        normed_tri = (layer_norm(triangle.astype(jnp.float32), -1) * gain_out).astype(jnp.bfloat16).reshape(LEN * LEN, CT)
        update = jnp.dot(normed_tri, out_weight, preferred_element_type=jnp.float32)
        gating = jax.nn.sigmoid(jnp.dot(normed, gate_weight, preferred_element_type=jnp.float32))
        updated = (pair_float + (gating * update).reshape(LEN, LEN, CP)).astype(jnp.bfloat16)
        updated_float = updated.astype(jnp.float32)
        symmetric = (updated_float + jnp.swapaxes(updated_float, 0, 1)).astype(jnp.bfloat16).reshape(LEN * LEN, CP)
        logits = jnp.dot(symmetric, head_weight, preferred_element_type=jnp.float32) + head_bias
        top_logit = lax.optimization_barrier(jnp.max(logits, axis=1, keepdims=True))
        log_total = jnp.log(lax.optimization_barrier(jnp.sum(jnp.exp(logits - top_logit), axis=1, keepdims=True))) + top_logit
        probability = jnp.exp(logits - log_total)
        bin_index = jnp.arange(NBINS, dtype=jnp.int32)
        target_hot = (crop_targets.reshape(-1)[:, None] == bin_index[None, :]).astype(jnp.float32)
        dlogits = (pair_mask[:, None] * (probability - target_hot)).astype(jnp.bfloat16)
        pair_term = jnp.dot(dlogits, head_weight.T, preferred_element_type=jnp.float32).reshape(LEN, LEN, CP)
        pair_grad = (pair_term + jnp.swapaxes(pair_term, 0, 1)).astype(jnp.bfloat16)
        head_part = jnp.dot(symmetric.T, dlogits, preferred_element_type=jnp.float32)
        bias_part = lax.optimization_barrier(jnp.sum(dlogits.astype(jnp.float32), axis=0))
        loss_part = jnp.sum(pair_mask * (log_total[:, 0] - lax.optimization_barrier(jnp.sum(target_hot * logits, axis=1))))
        count_part = jnp.sum(pair_mask)
        return (updated, pair_grad, head_part, bias_part, loss_part, count_part)
    updated, pair_grad, head_part, bias_part, loss_part, count_part = lax.map(one_crop, (pair, residue_mask, bin_targets))
    count = jnp.sum(count_part)
    head_grad = lax.optimization_barrier(jnp.sum(head_part, axis=0)) / count
    bias_grad = lax.optimization_barrier(jnp.sum(bias_part, axis=0)) / count
    mean_loss = jnp.reshape(jnp.sum(loss_part) / count, (1,))
    return (updated, pair_grad, head_grad, bias_grad, mean_loss)
```

```python
import jax
import jax.numpy as jnp
from jax import lax
from jax.sharding import PartitionSpec as P


def layer_norm(values, reduce_axis):
    average = jnp.mean(values, axis=reduce_axis, keepdims=True)
    centered = values - average
    variance = jnp.mean(centered * centered, axis=reduce_axis, keepdims=True)
    return centered * lax.rsqrt(variance + 1e-05)


def body(
    pair,
    residue_mask,
    bin_targets,
    gain_in,
    left_proj,
    left_gate,
    right_proj,
    right_gate,
    gate_weight,
    gain_out,
    out_weight,
    head_weight,
    head_bias,
):
    row_count = pair.shape[1]
    crop_pair = pair[0]
    targets = bin_targets[0]
    row_start = lax.axis_index("res") * row_count
    resolved = residue_mask[0].astype(jnp.float32)
    row_mask = lax.dynamic_slice_in_dim(resolved, row_start, row_count)
    pair_mask = row_mask[:, None] * resolved[None, :]
    pair_float = crop_pair.astype(jnp.float32)
    normed = (layer_norm(pair_float, 2) * gain_in).astype(jnp.bfloat16)
    mirror_targets = jnp.swapaxes(
        lax.all_to_all(targets, "res", split_axis=1, concat_axis=0, tiled=True), 0, 1
    )

    def factor(project_weight, gating_weight):
        projected = jnp.einsum(
            "rkd,dc->crk", normed, project_weight, preferred_element_type=jnp.float32
        )
        gated = jax.nn.sigmoid(
            jnp.einsum("rkd,dc->crk", normed, gating_weight, preferred_element_type=jnp.float32)
        )
        return (gated * projected * pair_mask[None]).astype(jnp.bfloat16)

    left_factor = factor(left_proj, left_gate)
    right_factor = factor(right_proj, right_gate)
    left_units, right_units = (
        lax.all_to_all(left_factor, "res", split_axis=0, concat_axis=1, tiled=True),
        lax.all_to_all(right_factor, "res", split_axis=0, concat_axis=1, tiled=True),
    )
    by_units = jnp.einsum(
        "cik,cjk->cij", left_units, right_units, preferred_element_type=jnp.float32
    ).astype(jnp.bfloat16)
    triangle_out = lax.all_to_all(by_units, "res", split_axis=1, concat_axis=0, tiled=True)
    normed_tri = (layer_norm(triangle_out.astype(jnp.float32), 0) * gain_out[:, None, None]).astype(
        jnp.bfloat16
    )
    update = jnp.einsum("crk,cd->rkd", normed_tri, out_weight, preferred_element_type=jnp.float32)
    gating = jax.nn.sigmoid(
        jnp.einsum("rkd,de->rke", normed, gate_weight, preferred_element_type=jnp.float32)
    )
    updated = (pair_float + gating * update).astype(jnp.bfloat16)
    mirrored = jnp.swapaxes(
        lax.all_to_all(updated, "res", split_axis=1, concat_axis=0, tiled=True), 0, 1
    )
    symmetric = (updated.astype(jnp.float32) + mirrored.astype(jnp.float32)).astype(jnp.bfloat16)
    logits = (
        jnp.einsum("rkd,dn->nrk", symmetric, head_weight, preferred_element_type=jnp.float32)
        + head_bias[:, None, None]
    )
    top_logit = jnp.max(logits, axis=0, keepdims=True)
    log_total = jnp.log(jnp.sum(jnp.exp(logits - top_logit), axis=0, keepdims=True)) + top_logit
    probability = jnp.exp(logits - log_total)
    bin_index = lax.broadcasted_iota(jnp.int32, (logits.shape[0], 1, 1), 0)
    target_hot = (targets[None] == bin_index).astype(jnp.float32)
    dlogits = (pair_mask[None] * (probability - target_hot)).astype(jnp.bfloat16)
    mirror_hot = (mirror_targets[None] == bin_index).astype(jnp.float32)
    mirror_dlogits = (pair_mask[None] * (probability - mirror_hot)).astype(jnp.bfloat16)
    pair_grad = jnp.einsum(
        "nrk,dn->rkd",
        jnp.concatenate([dlogits, mirror_dlogits], axis=0),
        jnp.concatenate([head_weight, head_weight], axis=1),
        preferred_element_type=jnp.float32,
    ).astype(jnp.bfloat16)
    head_part = jnp.einsum("rkd,nrk->dn", symmetric, dlogits, preferred_element_type=jnp.float32)
    bias_part = jnp.sum(dlogits.astype(jnp.float32), axis=(1, 2))
    loss_part = jnp.sum(pair_mask * (log_total[0] - jnp.sum(target_hot * logits, axis=0)))
    count_part = jnp.sum(pair_mask)
    head_total, bias_total, loss_total, count = lax.psum(
        (head_part, bias_part, loss_part, count_part), ("res", "rep")
    )
    mean_loss = jnp.reshape(loss_total / count, (1,))
    return (updated[None], pair_grad[None], head_total / count, bias_total / count, mean_loss)


def solution(mesh):
    return jax.shard_map(
        body,
        mesh=mesh,
        in_specs=(
            P("rep", "res", None, None),
            P("rep", None),
            P("rep", "res", None),
            P(),
            P(),
            P(),
            P(),
            P(),
            P(),
            P(),
            P(),
            P(),
            P(),
        ),
        out_specs=(P("rep", "res", None, None), P("rep", "res", None, None), P(), P(), P()),
        check_vma=False,
    )
```

```python
import jax
import jax.numpy as jnp
from jax import lax
from jax.sharding import PartitionSpec as P

CHUNKS = 2


def layer_norm(values, reduce_axis):
    average = jnp.mean(values, axis=reduce_axis, keepdims=True)
    centered = values - average
    variance = jnp.mean(centered * centered, axis=reduce_axis, keepdims=True)
    return centered * lax.rsqrt(variance + 1e-05)


def body(
    pair,
    residue_mask,
    bin_targets,
    gain_in,
    left_proj,
    left_gate,
    right_proj,
    right_gate,
    gate_weight,
    gain_out,
    out_weight,
    head_weight,
    head_bias,
):
    row_count = pair.shape[1]
    crop_pair = pair[0]
    targets = bin_targets[0]
    row_start = lax.axis_index("res") * row_count
    resolved = residue_mask[0].astype(jnp.float32)
    row_mask = lax.dynamic_slice_in_dim(resolved, row_start, row_count)
    pair_mask = row_mask[:, None] * resolved[None, :]
    pair_float = crop_pair.astype(jnp.float32)
    normed = (layer_norm(pair_float, 2) * gain_in).astype(jnp.bfloat16)
    mirror_targets = jnp.swapaxes(
        lax.all_to_all(targets, "res", split_axis=1, concat_axis=0, tiled=True), 0, 1
    )

    device_count = lax.axis_size("res")
    group = device_count // 2
    half_columns = crop_pair.shape[1] // 2
    me = lax.axis_index("res")
    half = me // group
    place = me % group
    groups = [list(range(group)), list(range(group, device_count))]
    across = [(d, (d + group) % device_count) for d in range(device_count)]
    own_start = half * half_columns
    other_start = (1 - half) * half_columns

    def factor(project_weight, gating_weight):
        projected = jnp.einsum(
            "rkd,dc->crk", normed, project_weight, preferred_element_type=jnp.float32
        )
        gated = jax.nn.sigmoid(
            jnp.einsum("rkd,dc->crk", normed, gating_weight, preferred_element_type=jnp.float32)
        )
        return (gated * projected * pair_mask[None]).astype(jnp.bfloat16)

    def in_half(values, split_axis, concat_axis):
        return lax.all_to_all(
            values,
            "res",
            split_axis=split_axis,
            concat_axis=concat_axis,
            axis_index_groups=groups,
            tiled=True,
        )

    unit_chunk = left_proj.shape[1] // CHUNKS
    spans = [slice(t * unit_chunk, (t + 1) * unit_chunk) for t in range(CHUNKS)]
    right_own = [in_half(factor(right_proj[:, t], right_gate[:, t]), 0, 1) for t in spans]
    right_other = [lax.ppermute(block, "res", across) for block in right_own]
    left_own = [in_half(factor(left_proj[:, t], left_gate[:, t]), 0, 1) for t in spans]
    gating = lax.optimization_barrier(
        jax.nn.sigmoid(
            jnp.einsum("rkd,de->rke", normed, gate_weight, preferred_element_type=jnp.float32)
        )
    )

    def updated_columns(right_blocks, start):
        parts = []
        for left_block, right_block in zip(left_own, right_blocks):
            product = jnp.einsum(
                "cik,cjk->cij", left_block, right_block, preferred_element_type=jnp.float32
            ).astype(jnp.bfloat16)
            parts.append(in_half(product, 1, 0))
        triangle_out = jnp.concatenate(parts, axis=0)
        normed_tri = (
            layer_norm(triangle_out.astype(jnp.float32), 0) * gain_out[:, None, None]
        ).astype(jnp.bfloat16)
        update = jnp.einsum(
            "crk,cd->rkd", normed_tri, out_weight, preferred_element_type=jnp.float32
        )
        gate_columns = lax.dynamic_slice_in_dim(gating, start, half_columns, 1)
        pair_columns = lax.dynamic_slice_in_dim(crop_pair, start, half_columns, 1)
        return (pair_columns.astype(jnp.float32) + gate_columns * update).astype(jnp.bfloat16)

    updated_own = updated_columns(right_own, own_start)
    mirrored = jnp.zeros((crop_pair.shape[1], row_count, crop_pair.shape[2]), jnp.bfloat16)
    mirrored = lax.dynamic_update_slice_in_dim(
        mirrored, in_half(updated_own, 1, 0), own_start, 0
    )
    updated_other = updated_columns(right_other, other_start)
    for shift in range(group):
        target = (place + shift) % group
        source = (place - shift) % group
        moves = [
            (d, (1 - d // group) * group + (d % group + shift) % group)
            for d in range(device_count)
        ]
        block = lax.dynamic_slice_in_dim(updated_other, target * row_count, row_count, 1)
        arrived = lax.ppermute(block, "res", moves)
        mirrored = lax.dynamic_update_slice_in_dim(
            mirrored, arrived, other_start + source * row_count, 0
        )
    updated = jnp.zeros_like(crop_pair)
    updated = lax.dynamic_update_slice_in_dim(updated, updated_own, own_start, 1)
    updated = lax.dynamic_update_slice_in_dim(updated, updated_other, other_start, 1)
    mirrored = jnp.swapaxes(mirrored, 0, 1)
    symmetric = (updated.astype(jnp.float32) + mirrored.astype(jnp.float32)).astype(jnp.bfloat16)
    logits = (
        jnp.einsum("rkd,dn->nrk", symmetric, head_weight, preferred_element_type=jnp.float32)
        + head_bias[:, None, None]
    )
    top_logit = jnp.max(logits, axis=0, keepdims=True)
    log_total = jnp.log(jnp.sum(jnp.exp(logits - top_logit), axis=0, keepdims=True)) + top_logit
    probability = jnp.exp(logits - log_total)
    bin_index = lax.broadcasted_iota(jnp.int32, (logits.shape[0], 1, 1), 0)
    target_hot = (targets[None] == bin_index).astype(jnp.float32)
    dlogits = (pair_mask[None] * (probability - target_hot)).astype(jnp.bfloat16)
    mirror_hot = (mirror_targets[None] == bin_index).astype(jnp.float32)
    mirror_dlogits = (pair_mask[None] * (probability - mirror_hot)).astype(jnp.bfloat16)
    pair_grad = jnp.einsum(
        "nrk,dn->rkd",
        jnp.concatenate([dlogits, mirror_dlogits], axis=0),
        jnp.concatenate([head_weight, head_weight], axis=1),
        preferred_element_type=jnp.float32,
    ).astype(jnp.bfloat16)
    head_part = jnp.einsum("rkd,nrk->dn", symmetric, dlogits, preferred_element_type=jnp.float32)
    bias_part = jnp.sum(dlogits.astype(jnp.float32), axis=(1, 2))
    loss_part = jnp.sum(pair_mask * (log_total[0] - jnp.sum(target_hot * logits, axis=0)))
    count_part = jnp.sum(pair_mask)
    head_total, bias_total, loss_total, count = lax.psum(
        (head_part, bias_part, loss_part, count_part), ("res", "rep")
    )
    mean_loss = jnp.reshape(loss_total / count, (1,))
    return (updated[None], pair_grad[None], head_total / count, bias_total / count, mean_loss)


def solution(mesh):
    return jax.shard_map(
        body,
        mesh=mesh,
        in_specs=(
            P("rep", "res", None, None),
            P("rep", None),
            P("rep", "res", None),
            P(),
            P(),
            P(),
            P(),
            P(),
            P(),
            P(),
            P(),
            P(),
            P(),
        ),
        out_specs=(P("rep", "res", None, None), P("rep", "res", None, None), P(), P(), P()),
        check_vma=False,
    )
```

```python
import jax
import jax.numpy as jnp
from jax import lax
from jax.sharding import PartitionSpec as P

CHUNKS = 2


def layer_norm(values, reduce_axis):
    average = jnp.mean(values, axis=reduce_axis, keepdims=True)
    centered = values - average
    variance = jnp.mean(centered * centered, axis=reduce_axis, keepdims=True)
    return centered * lax.rsqrt(variance + 1e-05)


def total_over(values, axis_name):
    size = lax.axis_size(axis_name)
    if size & (size - 1):
        return lax.psum(values, axis_name)
    step = 1
    while step < size:
        moves = [(d, d ^ step) for d in range(size)]
        values = values + lax.ppermute(values, axis_name, moves)
        step *= 2
    return values


def body(
    pair,
    residue_mask,
    bin_targets,
    gain_in,
    left_proj,
    left_gate,
    right_proj,
    right_gate,
    gate_weight,
    gain_out,
    out_weight,
    head_weight,
    head_bias,
):
    row_count = pair.shape[1]
    crop_pair = pair[0]
    targets = bin_targets[0]
    row_start = lax.axis_index("res") * row_count
    resolved = residue_mask[0].astype(jnp.float32)
    row_mask = lax.dynamic_slice_in_dim(resolved, row_start, row_count)
    pair_mask = row_mask[:, None] * resolved[None, :]
    pair_float = crop_pair.astype(jnp.float32)
    normed = (layer_norm(pair_float, 2) * gain_in).astype(jnp.bfloat16)
    mirror_targets = jnp.swapaxes(
        lax.all_to_all(targets, "res", split_axis=1, concat_axis=0, tiled=True), 0, 1
    )

    device_count = lax.axis_size("res")
    group = device_count // 2
    half_columns = crop_pair.shape[1] // 2
    me = lax.axis_index("res")
    half = me // group
    place = me % group
    groups = [list(range(group)), list(range(group, device_count))]
    across = [(d, (d + group) % device_count) for d in range(device_count)]
    own_start = half * half_columns
    other_start = (1 - half) * half_columns

    def factor(project_weight, gating_weight):
        projected = jnp.einsum(
            "rkd,dc->crk", normed, project_weight, preferred_element_type=jnp.float32
        )
        gated = jax.nn.sigmoid(
            jnp.einsum("rkd,dc->crk", normed, gating_weight, preferred_element_type=jnp.float32)
        )
        return (gated * projected * pair_mask[None]).astype(jnp.bfloat16)

    def in_half(values, split_axis, concat_axis):
        return lax.all_to_all(
            values,
            "res",
            split_axis=split_axis,
            concat_axis=concat_axis,
            axis_index_groups=groups,
            tiled=True,
        )

    unit_chunk = left_proj.shape[1] // CHUNKS
    spans = [slice(t * unit_chunk, (t + 1) * unit_chunk) for t in range(CHUNKS)]
    tie = lax.optimization_barrier
    right_factor = tie(factor(right_proj, right_gate))
    left_factor = factor(left_proj, left_gate)
    right_own = []
    right_other = []
    for t in spans:
        block = right_factor[t]
        if right_own:
            block, right_own[-1] = tie((block, right_own[-1]))
        right_own.append(in_half(block, 0, 1))
    left_factor, right_own[-1] = tie((left_factor, right_own[-1]))
    right_other = [lax.ppermute(block, "res", across) for block in right_own]
    left_own = [in_half(left_factor[t], 0, 1) for t in spans]
    gating = jax.nn.sigmoid(
        jnp.einsum("rkd,de->rke", normed, gate_weight, preferred_element_type=jnp.float32)
    )

    def products(right_blocks):
        return [
            jnp.einsum(
                "cik,cjk->cij", left_block, right_block, preferred_element_type=jnp.float32
            ).astype(jnp.bfloat16)
            for left_block, right_block in zip(left_own, right_blocks)
        ]

    def updated_columns(own_products, start):
        parts = [in_half(product, 1, 0) for product in own_products]
        triangle_out = jnp.concatenate(parts, axis=0)
        normed_tri = (
            layer_norm(triangle_out.astype(jnp.float32), 0) * gain_out[:, None, None]
        ).astype(jnp.bfloat16)
        update = jnp.einsum(
            "crk,cd->rkd", normed_tri, out_weight, preferred_element_type=jnp.float32
        )
        gate_columns = lax.dynamic_slice_in_dim(gating, start, half_columns, 1)
        pair_columns = lax.dynamic_slice_in_dim(crop_pair, start, half_columns, 1)
        return (pair_columns.astype(jnp.float32) + gate_columns * update).astype(jnp.bfloat16)

    own_products, gating, mirror_targets, right_other[0] = tie(
        (products(right_own), gating, mirror_targets, right_other[0])
    )
    updated_own = updated_columns(own_products, own_start)
    updated_own, right_other[-1] = tie((updated_own, right_other[-1]))
    mirrored = jnp.zeros((crop_pair.shape[1], row_count, crop_pair.shape[2]), jnp.bfloat16)
    mirrored = lax.dynamic_update_slice_in_dim(
        mirrored, in_half(updated_own, 1, 0), own_start, 0
    )
    updated_other = updated_columns(products(right_other), other_start)
    for shift in range(group):
        target = (place + shift) % group
        source = (place - shift) % group
        moves = [
            (d, (1 - d // group) * group + (d % group + shift) % group)
            for d in range(device_count)
        ]
        block = lax.dynamic_slice_in_dim(updated_other, target * row_count, row_count, 1)
        arrived = lax.ppermute(block, "res", moves)
        mirrored = lax.dynamic_update_slice_in_dim(
            mirrored, arrived, other_start + source * row_count, 0
        )
    updated = jnp.zeros_like(crop_pair)
    updated = lax.dynamic_update_slice_in_dim(updated, updated_own, own_start, 1)
    updated = lax.dynamic_update_slice_in_dim(updated, updated_other, other_start, 1)
    mirrored = jnp.swapaxes(mirrored, 0, 1)
    symmetric = (updated.astype(jnp.float32) + mirrored.astype(jnp.float32)).astype(jnp.bfloat16)
    logits = (
        jnp.einsum("rkd,dn->nrk", symmetric, head_weight, preferred_element_type=jnp.float32)
        + head_bias[:, None, None]
    )
    top_logit = jnp.max(logits, axis=0, keepdims=True)
    log_total = jnp.log(jnp.sum(jnp.exp(logits - top_logit), axis=0, keepdims=True)) + top_logit
    probability = jnp.exp(logits - log_total)
    bin_index = lax.broadcasted_iota(jnp.int32, (logits.shape[0], 1, 1), 0)
    target_hot = (targets[None] == bin_index).astype(jnp.float32)
    dlogits = (pair_mask[None] * (probability - target_hot)).astype(jnp.bfloat16)
    mirror_hot = (mirror_targets[None] == bin_index).astype(jnp.float32)
    mirror_dlogits = (pair_mask[None] * (probability - mirror_hot)).astype(jnp.bfloat16)
    pair_grad = jnp.einsum(
        "nrk,dn->rkd",
        jnp.concatenate([dlogits, mirror_dlogits], axis=0),
        jnp.concatenate([head_weight, head_weight], axis=1),
        preferred_element_type=jnp.float32,
    ).astype(jnp.bfloat16)
    head_part = jnp.einsum("rkd,nrk->dn", symmetric, dlogits, preferred_element_type=jnp.float32)
    bias_part = jnp.sum(dlogits.astype(jnp.float32), axis=(1, 2))
    loss_part = jnp.sum(pair_mask * (log_total[0] - jnp.sum(target_hot * logits, axis=0)))
    count_part = jnp.sum(pair_mask)
    head_shape = head_part.shape
    packed = jnp.concatenate(
        [
            head_part.reshape(-1, 128),
            jnp.pad(bias_part, (0, 128 - bias_part.shape[0]))[None],
            jnp.pad(jnp.stack([loss_part, count_part]), (0, 126))[None],
        ],
        axis=0,
    )
    packed = total_over(total_over(packed, "res"), "rep")
    head_total = packed[:-2].reshape(head_shape)
    bias_total = packed[-2, : bias_part.shape[0]]
    loss_total, count = packed[-1, 0], packed[-1, 1]
    mean_loss = jnp.reshape(loss_total / count, (1,))
    return (updated[None], pair_grad[None], head_total / count, bias_total / count, mean_loss)


def solution(mesh):
    return jax.shard_map(
        body,
        mesh=mesh,
        in_specs=(
            P("rep", "res", None, None),
            P("rep", None),
            P("rep", "res", None),
            P(),
            P(),
            P(),
            P(),
            P(),
            P(),
            P(),
            P(),
            P(),
            P(),
        ),
        out_specs=(P("rep", "res", None, None), P("rep", "res", None, None), P(), P(), P()),
        check_vma=False,
    )
```

```python
import jax
import jax.numpy as jnp
from jax import lax
from jax.sharding import PartitionSpec as P

CHUNKS = 2


def layer_norm(values, reduce_axis):
    average = jnp.mean(values, axis=reduce_axis, keepdims=True)
    centered = values - average
    variance = jnp.mean(centered * centered, axis=reduce_axis, keepdims=True)
    return centered * lax.rsqrt(variance + 1e-05)


def total_over(values, axis_name):
    size = lax.axis_size(axis_name)
    if size & (size - 1):
        return lax.psum(values, axis_name)
    step = 1
    while step < size:
        moves = [(d, d ^ step) for d in range(size)]
        values = values + lax.ppermute(values, axis_name, moves)
        step *= 2
    return values


def body(
    pair,
    residue_mask,
    bin_targets,
    gain_in,
    left_proj,
    left_gate,
    right_proj,
    right_gate,
    gate_weight,
    gain_out,
    out_weight,
    head_weight,
    head_bias,
):
    row_count = pair.shape[1]
    crop_pair = pair[0]
    targets = bin_targets[0]
    row_start = lax.axis_index("res") * row_count
    resolved = residue_mask[0].astype(jnp.float32)
    row_mask = lax.dynamic_slice_in_dim(resolved, row_start, row_count)
    pair_mask = row_mask[:, None] * resolved[None, :]
    pair_float = crop_pair.astype(jnp.float32)
    normed = (layer_norm(pair_float, 2) * gain_in).astype(jnp.bfloat16)
    mirror_targets = jnp.swapaxes(
        lax.all_to_all(targets, "res", split_axis=1, concat_axis=0, tiled=True), 0, 1
    )

    device_count = lax.axis_size("res")
    group = device_count // 2
    half_columns = crop_pair.shape[1] // 2
    me = lax.axis_index("res")
    half = me // group
    place = me % group
    groups = [list(range(group)), list(range(group, device_count))]
    across = [(d, (d + group) % device_count) for d in range(device_count)]
    own_start = half * half_columns
    other_start = (1 - half) * half_columns

    def factor(project_weight, gating_weight):
        projected = jnp.einsum(
            "rkd,dc->crk", normed, project_weight, preferred_element_type=jnp.float32
        )
        gated = jax.nn.sigmoid(
            jnp.einsum("rkd,dc->crk", normed, gating_weight, preferred_element_type=jnp.float32)
        )
        return (gated * projected * pair_mask[None]).astype(jnp.bfloat16)

    def in_half(values, split_axis, concat_axis):
        return lax.all_to_all(
            values,
            "res",
            split_axis=split_axis,
            concat_axis=concat_axis,
            axis_index_groups=groups,
            tiled=True,
        )

    tie = lax.optimization_barrier
    right_own = in_half(factor(right_proj, right_gate), 0, 1)
    left_factor, right_own = tie((factor(left_proj, left_gate), right_own))
    unit_chunk = right_own.shape[0] // CHUNKS
    spans = [slice(t * unit_chunk, (t + 1) * unit_chunk) for t in range(CHUNKS)]
    right_other = [lax.ppermute(right_own[t], "res", across) for t in spans]
    left_own = in_half(left_factor, 0, 1)
    gating = jax.nn.sigmoid(
        jnp.einsum("rkd,de->rke", normed, gate_weight, preferred_element_type=jnp.float32)
    )

    def product(left_block, right_block):
        return jnp.einsum(
            "cik,cjk->cij", left_block, right_block, preferred_element_type=jnp.float32
        ).astype(jnp.bfloat16)

    def updated_columns(triangle_out, start):
        normed_tri = (
            layer_norm(triangle_out.astype(jnp.float32), 0) * gain_out[:, None, None]
        ).astype(jnp.bfloat16)
        update = jnp.einsum(
            "crk,cd->rkd", normed_tri, out_weight, preferred_element_type=jnp.float32
        )
        gate_columns = lax.dynamic_slice_in_dim(gating, start, half_columns, 1)
        pair_columns = lax.dynamic_slice_in_dim(crop_pair, start, half_columns, 1)
        return (pair_columns.astype(jnp.float32) + gate_columns * update).astype(jnp.bfloat16)

    own_product, gating, mirror_targets, right_other[0] = tie(
        (product(left_own, right_own), gating, mirror_targets, right_other[0])
    )
    own_part = in_half(own_product, 1, 0)
    first_part = in_half(product(left_own[spans[0]], right_other[0]), 1, 0)
    own_part, first_part, right_other[1] = tie((own_part, first_part, right_other[1]))
    updated_own = updated_columns(own_part, own_start)
    second_part = in_half(product(left_own[spans[1]], right_other[1]), 1, 0)
    other_part = jnp.concatenate(
        [
            part.reshape((group, unit_chunk) + part.shape[1:])
            for part in (first_part, second_part)
        ],
        axis=1,
    ).reshape(own_part.shape)
    mirrored = jnp.zeros((crop_pair.shape[1], row_count, crop_pair.shape[2]), jnp.bfloat16)
    mirrored = lax.dynamic_update_slice_in_dim(
        mirrored, in_half(updated_own, 1, 0), own_start, 0
    )
    updated_other = updated_columns(other_part, other_start)
    for shift in range(group):
        target = (place + shift) % group
        source = (place - shift) % group
        moves = [
            (d, (1 - d // group) * group + (d % group + shift) % group)
            for d in range(device_count)
        ]
        block = lax.dynamic_slice_in_dim(updated_other, target * row_count, row_count, 1)
        arrived = lax.ppermute(block, "res", moves)
        mirrored = lax.dynamic_update_slice_in_dim(
            mirrored, arrived, other_start + source * row_count, 0
        )
    updated = jnp.zeros_like(crop_pair)
    updated = lax.dynamic_update_slice_in_dim(updated, updated_own, own_start, 1)
    updated = lax.dynamic_update_slice_in_dim(updated, updated_other, other_start, 1)
    mirrored = jnp.swapaxes(mirrored, 0, 1)
    symmetric = (updated.astype(jnp.float32) + mirrored.astype(jnp.float32)).astype(jnp.bfloat16)
    logits = (
        jnp.einsum("rkd,dn->nrk", symmetric, head_weight, preferred_element_type=jnp.float32)
        + head_bias[:, None, None]
    )
    top_logit = jnp.max(logits, axis=0, keepdims=True)
    log_total = jnp.log(jnp.sum(jnp.exp(logits - top_logit), axis=0, keepdims=True)) + top_logit
    probability = jnp.exp(logits - log_total)
    bin_index = lax.broadcasted_iota(jnp.int32, (logits.shape[0], 1, 1), 0)
    target_hot = (targets[None] == bin_index).astype(jnp.float32)
    dlogits = (pair_mask[None] * (probability - target_hot)).astype(jnp.bfloat16)
    mirror_hot = (mirror_targets[None] == bin_index).astype(jnp.float32)
    mirror_dlogits = (pair_mask[None] * (probability - mirror_hot)).astype(jnp.bfloat16)
    pair_grad = jnp.einsum(
        "nrk,dn->rkd",
        jnp.concatenate([dlogits, mirror_dlogits], axis=0),
        jnp.concatenate([head_weight, head_weight], axis=1),
        preferred_element_type=jnp.float32,
    ).astype(jnp.bfloat16)
    head_part = jnp.einsum("rkd,nrk->dn", symmetric, dlogits, preferred_element_type=jnp.float32)
    bias_part = jnp.sum(dlogits.astype(jnp.float32), axis=(1, 2))
    loss_part = jnp.sum(pair_mask * (log_total[0] - jnp.sum(target_hot * logits, axis=0)))
    count_part = jnp.sum(pair_mask)
    head_shape = head_part.shape
    packed = jnp.concatenate(
        [
            head_part.reshape(-1, 128),
            jnp.pad(bias_part, (0, 128 - bias_part.shape[0]))[None],
            jnp.pad(jnp.stack([loss_part, count_part]), (0, 126))[None],
        ],
        axis=0,
    )
    packed = total_over(total_over(packed, "res"), "rep")
    head_total = packed[:-2].reshape(head_shape)
    bias_total = packed[-2, : bias_part.shape[0]]
    loss_total, count = packed[-1, 0], packed[-1, 1]
    mean_loss = jnp.reshape(loss_total / count, (1,))
    return (updated[None], pair_grad[None], head_total / count, bias_total / count, mean_loss)


def solution(mesh):
    return jax.shard_map(
        body,
        mesh=mesh,
        in_specs=(
            P("rep", "res", None, None),
            P("rep", None),
            P("rep", "res", None),
            P(),
            P(),
            P(),
            P(),
            P(),
            P(),
            P(),
            P(),
            P(),
            P(),
        ),
        out_specs=(P("rep", "res", None, None), P("rep", "res", None, None), P(), P(), P()),
        check_vma=False,
    )
```

```python
import jax
import jax.numpy as jnp
from jax import lax
from jax.sharding import PartitionSpec as P


def layer_norm(values, reduce_axis):
    average = jnp.mean(values, axis=reduce_axis, keepdims=True)
    centered = values - average
    variance = jnp.mean(centered * centered, axis=reduce_axis, keepdims=True)
    return centered * lax.rsqrt(variance + 1e-05)


def total_over(values, axis_name):
    size = lax.axis_size(axis_name)
    if size & (size - 1):
        return lax.psum(values, axis_name)
    step = 1
    while step < size:
        moves = [(d, d ^ step) for d in range(size)]
        values = values + lax.ppermute(values, axis_name, moves)
        step *= 2
    return values


def body(
    pair,
    residue_mask,
    bin_targets,
    gain_in,
    left_proj,
    left_gate,
    right_proj,
    right_gate,
    gate_weight,
    gain_out,
    out_weight,
    head_weight,
    head_bias,
):
    row_count = pair.shape[1]
    crop_pair = pair[0]
    targets = bin_targets[0]
    row_start = lax.axis_index("res") * row_count
    resolved = residue_mask[0].astype(jnp.float32)
    row_mask = lax.dynamic_slice_in_dim(resolved, row_start, row_count)
    pair_mask = row_mask[:, None] * resolved[None, :]
    pair_float = crop_pair.astype(jnp.float32)
    normed = (layer_norm(pair_float, 2) * gain_in).astype(jnp.bfloat16)
    mirror_targets = jnp.swapaxes(
        lax.all_to_all(targets, "res", split_axis=1, concat_axis=0, tiled=True), 0, 1
    )

    def factor(project_weight, gating_weight):
        projected = jnp.einsum(
            "rkd,dc->crk", normed, project_weight, preferred_element_type=jnp.float32
        )
        gated = jax.nn.sigmoid(
            jnp.einsum("rkd,dc->crk", normed, gating_weight, preferred_element_type=jnp.float32)
        )
        return (gated * projected * pair_mask[None]).astype(jnp.bfloat16)

    left_factor = factor(left_proj, left_gate)
    right_factor = factor(right_proj, right_gate)
    left_units, right_units = (
        lax.all_to_all(left_factor, "res", split_axis=0, concat_axis=1, tiled=True),
        lax.all_to_all(right_factor, "res", split_axis=0, concat_axis=1, tiled=True),
    )
    by_units = jnp.einsum(
        "cik,cjk->cij", left_units, right_units, preferred_element_type=jnp.float32
    ).astype(jnp.bfloat16)
    triangle_out = lax.all_to_all(by_units, "res", split_axis=1, concat_axis=0, tiled=True)
    normed_tri = (layer_norm(triangle_out.astype(jnp.float32), 0) * gain_out[:, None, None]).astype(
        jnp.bfloat16
    )
    update = jnp.einsum("crk,cd->rkd", normed_tri, out_weight, preferred_element_type=jnp.float32)
    gating = jax.nn.sigmoid(
        jnp.einsum("rkd,de->rke", normed, gate_weight, preferred_element_type=jnp.float32)
    )
    updated = (pair_float + gating * update).astype(jnp.bfloat16)
    mirrored = jnp.swapaxes(
        lax.all_to_all(updated, "res", split_axis=1, concat_axis=0, tiled=True), 0, 1
    )
    symmetric = (updated.astype(jnp.float32) + mirrored.astype(jnp.float32)).astype(jnp.bfloat16)
    logits = (
        jnp.einsum("rkd,dn->nrk", symmetric, head_weight, preferred_element_type=jnp.float32)
        + head_bias[:, None, None]
    )
    top_logit = jnp.max(logits, axis=0, keepdims=True)
    log_total = jnp.log(jnp.sum(jnp.exp(logits - top_logit), axis=0, keepdims=True)) + top_logit
    probability = jnp.exp(logits - log_total)
    bin_index = lax.broadcasted_iota(jnp.int32, (logits.shape[0], 1, 1), 0)
    target_hot = (targets[None] == bin_index).astype(jnp.float32)
    dlogits = (pair_mask[None] * (probability - target_hot)).astype(jnp.bfloat16)
    mirror_hot = (mirror_targets[None] == bin_index).astype(jnp.float32)
    mirror_dlogits = (pair_mask[None] * (probability - mirror_hot)).astype(jnp.bfloat16)
    pair_grad = jnp.einsum(
        "nrk,dn->rkd",
        jnp.concatenate([dlogits, mirror_dlogits], axis=0),
        jnp.concatenate([head_weight, head_weight], axis=1),
        preferred_element_type=jnp.float32,
    ).astype(jnp.bfloat16)
    head_part = jnp.einsum("rkd,nrk->dn", symmetric, dlogits, preferred_element_type=jnp.float32)
    bias_part = jnp.sum(dlogits.astype(jnp.float32), axis=(1, 2))
    loss_part = jnp.sum(pair_mask * (log_total[0] - jnp.sum(target_hot * logits, axis=0)))
    count_part = jnp.sum(pair_mask)
    head_shape = head_part.shape
    packed = jnp.concatenate(
        [
            head_part.reshape(-1, 128),
            jnp.pad(bias_part, (0, 128 - bias_part.shape[0]))[None],
            jnp.pad(jnp.stack([loss_part, count_part]), (0, 126))[None],
        ],
        axis=0,
    )
    packed = total_over(total_over(packed, "res"), "rep")
    head_total = packed[:-2].reshape(head_shape)
    bias_total = packed[-2, : bias_part.shape[0]]
    loss_total, count = packed[-1, 0], packed[-1, 1]
    mean_loss = jnp.reshape(loss_total / count, (1,))
    return (updated[None], pair_grad[None], head_total / count, bias_total / count, mean_loss)


def solution(mesh):
    return jax.shard_map(
        body,
        mesh=mesh,
        in_specs=(
            P("rep", "res", None, None),
            P("rep", None),
            P("rep", "res", None),
            P(),
            P(),
            P(),
            P(),
            P(),
            P(),
            P(),
            P(),
            P(),
            P(),
        ),
        out_specs=(P("rep", "res", None, None), P("rep", "res", None, None), P(), P(), P()),
        check_vma=False,
    )
```
